128 devices in a mesh: prefix: 16 (over z, x), row: 8 (over y, core).
Axes of the slice: x: 4, y: 4, z: 4, core: 2. Of those that a mesh axis runs over, the one named last changes fastest.
Arguments:
- queries: bfloat16 [1024, 8192], P(('prefix', 'row')), may hold values from -32 to 32
- prefix_ids: int32 [1024], P(('prefix', 'row')), may hold values from 0 to 15, as said below
- prefix_lengths: int32 [16], P('prefix'), may hold values from 1 to 16384, 65536 in all
- prefix_keys: bfloat16 [16, 8, 16384, 128], P('prefix', None, 'row'), may hold values from -12 to 12
- prefix_values: bfloat16 [16, 8, 16384, 128], P('prefix', None, 'row'), may hold values from -6 to 6
- suffix_keys: bfloat16 [1024, 8, 512, 128], P(('prefix', 'row')), may hold values from -12 to 12
- suffix_values: bfloat16 [1024, 8, 512, 128], P(('prefix', 'row')), may hold values from -6 to 6
- suffix_lengths: int32 [1024], P(('prefix', 'row')), may hold values from 1 to 512, 393216 in all
Outputs:
- attended: bfloat16 [1024, 8192], P(('prefix', 'row'))
The draws below stay inside these ranges and needn't reach their ends.
Inputs may be any that keep to these rules, and one draw needn't show every extreme that they name: `prefix_ids`: each block of 8 requests held by one device names any prefix at most 2 times, and one prefix is named exactly 2 times in every block.
All inputs are finite; a program needn't handle non-finite values. No bound on the sum of `prefix_lengths` or of `suffix_lengths` on one device may be relied on, other than what follows from the above.
Results may differ from the reference program's by a relative error of at most 0.01.
Values may be sent and summed in bfloat16 or wider, within the bound.
No kernel may reach another device: no remote copies, remote signals or barrier semaphores. Data moves between devices by JAX's collectives and lax.ppermute only.
A program may use at most 320 MiB of HBM per device.

```python
import math
import jax
import jax.numpy as jnp
import numpy as np
from jax import lax

HEADS = 64
KV_HEADS = 8
HD = 128
ROWS_DEV = 8
SLEN = 512
PLEN = 16384
CAP = 2
PREFIXES = 16
ROWS = 1024
N_PREFIX = 16
N_ROW = 8


def draw_queries(key, part):
    key = jax.random.fold_in(key, 1)
    return jnp.clip(jax.random.normal(key, (ROWS, HEADS * HD), jnp.float32), -6.0, 6.0).astype(jnp.bfloat16)


def draw_prefix_keys(key, part):
    key = jax.random.fold_in(key, 2)
    return jnp.clip(jax.random.normal(key, (PREFIXES, KV_HEADS, PLEN, HD), jnp.float32), -6.0, 6.0).astype(jnp.bfloat16)


def draw_suffix_keys(key, part):
    key = jax.random.fold_in(key, 3)
    return jnp.clip(jax.random.normal(key, (ROWS, KV_HEADS, SLEN, HD), jnp.float32), -6.0, 6.0).astype(jnp.bfloat16)


def draw_prefix_ids(key, part):
    key = jax.random.fold_in(key, 5)
    favored_key, block_key = jax.random.split(key)
    favored = jax.random.randint(favored_key, (), 0, PREFIXES, dtype=jnp.int32)

    def one_block(block_seed):
        pool_key, shuffle_key = jax.random.split(block_seed)
        pool_index = jax.random.permutation(pool_key, CAP * (PREFIXES - 1))[:ROWS_DEV - CAP].astype(jnp.int32)
        others = (favored + 1 + pool_index % (PREFIXES - 1)) % PREFIXES
        chosen_ids = jnp.concatenate([jnp.full((CAP,), favored, jnp.int32), others.astype(jnp.int32)])
        return jax.random.permutation(shuffle_key, chosen_ids)
    blocks_ids = jax.vmap(one_block)(jax.random.split(block_key, ROWS // ROWS_DEV))
    return blocks_ids.reshape(ROWS).astype(jnp.int32)


def shard_levels(rng, dims, cuts, low, high):
    factor_of, own = 1.0, jax.random.fold_in(rng, 6)
    for axis_at, parts in cuts:
        heights = jnp.exp(jax.random.uniform(jax.random.fold_in(own, axis_at), (parts,), jnp.float32, low / len(cuts), high / len(cuts)))
        factor_of = factor_of * jnp.repeat(heights, dims[axis_at] // parts).reshape([-1 if axis == axis_at else 1 for axis in range(len(dims))])
    return factor_of


def profile(number_of, total, reach, skew):
    weights = [(1 << 20) // math.isqrt(standing ** skew) + 1 for standing in range(2, number_of + 1)]
    spare, given = total - reach - (number_of - 1), [1] * (number_of - 1)
    while spare > 0:
        free = [i for i in range(number_of - 1) if given[i] < reach]
        whole, left = sum([weights[i] for i in free]), spare
        for i in free:
            more = min(reach - given[i], max(1, left * weights[i] // whole), spare)
            given[i] = given[i] + more
            spare = spare - more
    return np.array([reach] + given)


def ragged_sizes(stream_key, number_of, total, bound, slope):
    if number_of == 2:
        one = jax.random.randint(stream_key, (), max(1, total - bound), min(bound, total - 1) + 1)
        return jnp.stack([one, total - one])
    lengths = jnp.asarray(profile(number_of, total, bound, slope), jnp.int32)
    couples = (number_of - 1) // 2
    donor, receiver = lengths[1:1 + 2 * couples:2], lengths[2:2 + 2 * couples:2]
    slack = jnp.minimum(donor - 1, bound - receiver)
    moved = jax.random.randint(jax.random.fold_in(stream_key, 1), (couples,), 0, 1 << 20) % (slack + 1)
    lengths = lengths.at[1:1 + 2 * couples:2].set(donor - moved).at[2:2 + 2 * couples:2].set(receiver + moved)
    return lengths[jax.random.permutation(jax.random.fold_in(stream_key, 2), number_of)]


def normal_values(own_key, shape, deviation, limit, shards=(), kind=jnp.bfloat16):
    entries = jax.random.normal(own_key, shape, jnp.float32) * deviation
    if len(shards) > 0:
        entries = shard_levels(own_key, shape, shards, -0.22, 0.18) * entries
    return jnp.clip(entries, min=-limit, max=limit).astype(kind)


def setup_inputs(seed: int = 0) -> dict:
    key_of = jax.random.split(jax.random.key(seed), 9)
    return {
        "queries": draw_queries(jax.random.fold_in(key_of[8], 71), 0),
        "prefix_ids": draw_prefix_ids(jax.random.fold_in(key_of[8], 71), 0),
        "prefix_lengths": ragged_sizes(key_of[2], PREFIXES, PREFIXES * PLEN // 4, PLEN, 1).astype(jnp.int32),
        "prefix_keys": draw_prefix_keys(jax.random.fold_in(key_of[8], 71), 0),
        "prefix_values": normal_values(key_of[4], (PREFIXES, KV_HEADS, PLEN, HD), 1.0, 6.0, ((0, 16), (2, 8))),
        "suffix_keys": draw_suffix_keys(jax.random.fold_in(key_of[8], 71), 0),
        "suffix_values": normal_values(key_of[6], (ROWS, KV_HEADS, SLEN, HD), 1.0, 6.0, ((0, 128),)),
        "suffix_lengths": ragged_sizes(key_of[7], ROWS, ROWS * SLEN * 3 // 4, SLEN, 1).astype(jnp.int32),
    }


MASKED = -1e+30

def softmax_parts(scores, is_valid):
    row_peak = lax.optimization_barrier(jnp.max(jnp.where(is_valid, scores, MASKED), axis=-1))
    weights = jnp.where(is_valid, jnp.exp(scores - row_peak[..., None]), 0.0)
    row_total = lax.optimization_barrier(jnp.sum(weights, axis=-1))
    rounded = lax.optimization_barrier(weights.astype(jnp.bfloat16)).astype(jnp.float32)
    return (row_peak, row_total, rounded)

def reference(queries, prefix_ids, prefix_lengths, prefix_keys, prefix_values, suffix_keys, suffix_values, suffix_lengths):
    groups = HEADS // KV_HEADS
    scaling = 1.0 / math.sqrt(HD)
    block_span = PLEN // N_ROW
    row_bound = CAP * N_PREFIX * N_ROW
    positions = jnp.arange(PLEN, dtype=jnp.int32).reshape(N_ROW, block_span)
    grouped_all = queries.astype(jnp.float32).reshape(ROWS, KV_HEADS, groups, HD)

    def one_prefix(carried, prefix_index):
        peak_all, total_all, output_all = carried
        chosen = jnp.argsort((prefix_ids != prefix_index).astype(jnp.int32)).astype(jnp.int32)[:row_bound]
        matched = prefix_ids[chosen] == prefix_index
        prefix_length = lax.dynamic_index_in_dim(prefix_lengths, prefix_index, 0, keepdims=False)
        is_valid = (positions < prefix_length)[None, None]
        shared_keys = lax.dynamic_index_in_dim(prefix_keys, prefix_index, 0, keepdims=False).astype(jnp.float32)
        shared_values = lax.dynamic_index_in_dim(prefix_values, prefix_index, 0, keepdims=False).astype(jnp.float32)
        picked = grouped_all[chosen]
        peaks, totals, outputs = ([], [], [])
        for kv_index in range(KV_HEADS):
            scores = jnp.einsum('rgd,td->rgt', picked[:, kv_index], shared_keys[kv_index], precision=lax.Precision.HIGHEST) * scaling
            block_peak, block_total, rounded = softmax_parts(scores.reshape(row_bound, groups, N_ROW, block_span), is_valid)
            block_output = jnp.einsum('rgbt,btd->rgbd', rounded, shared_values[kv_index].reshape(N_ROW, block_span, HD), precision=lax.Precision.HIGHEST)
            prefix_peak = lax.optimization_barrier(jnp.max(block_peak, axis=-1))
            factor = jnp.exp(block_peak - prefix_peak[..., None])
            peaks.append(prefix_peak)
            totals.append(lax.optimization_barrier(jnp.sum(block_total * factor, axis=-1)))
            outputs.append(lax.optimization_barrier(jnp.sum(block_output * factor[..., None], axis=2)))
        new_peak = jnp.stack(peaks, 1).reshape(row_bound, HEADS)
        new_total = jnp.stack(totals, 1).reshape(row_bound, HEADS)
        new_output = jnp.stack(outputs, 1).reshape(row_bound, HEADS, HD)
        peak_all = peak_all.at[chosen].set(jnp.where(matched[:, None], new_peak, peak_all[chosen]))
        total_all = total_all.at[chosen].set(jnp.where(matched[:, None], new_total, total_all[chosen]))
        output_all = output_all.at[chosen].set(jnp.where(matched[:, None, None], new_output, output_all[chosen]))
        return ((peak_all, total_all, output_all), None)
    start_state = (jnp.zeros((ROWS, HEADS), jnp.float32), jnp.zeros((ROWS, HEADS), jnp.float32), jnp.zeros((ROWS, HEADS, HD), jnp.float32))
    (peak_all, total_all, output_all), _ = lax.scan(one_prefix, start_state, jnp.arange(PREFIXES, dtype=jnp.int32))
    slot_index = jnp.arange(SLEN, dtype=jnp.int32)

    def finish(row_item):
        query_row, suffix_length, own_keys, own_values, prefix_peak, prefix_total, prefix_output = row_item
        grouped = query_row.astype(jnp.float32).reshape(KV_HEADS, groups, HD)
        scores = jnp.einsum('kgd,ktd->kgt', grouped, own_keys.astype(jnp.float32), precision=lax.Precision.HIGHEST) * scaling
        is_valid = (slot_index < suffix_length)[None, None]
        suffix_peak, suffix_total, rounded = softmax_parts(scores, is_valid)
        suffix_output = jnp.einsum('kgt,ktd->kgd', rounded, own_values.astype(jnp.float32), precision=lax.Precision.HIGHEST)
        suffix_peak = suffix_peak.reshape(HEADS)
        suffix_total = suffix_total.reshape(HEADS)
        suffix_output = suffix_output.reshape(HEADS, HD)
        highest = jnp.maximum(prefix_peak, suffix_peak)
        prefix_scale = jnp.exp(prefix_peak - highest)
        suffix_scale = jnp.exp(suffix_peak - highest)
        numerator = prefix_scale[:, None] * prefix_output + suffix_scale[:, None] * suffix_output
        denominator = prefix_scale * prefix_total + suffix_scale * suffix_total
        return (numerator / denominator[:, None]).reshape(HEADS * HD).astype(jnp.bfloat16)
    return lax.map(finish, (queries, suffix_lengths, suffix_keys, suffix_values, peak_all, total_all, output_all))
```

```python
import functools
import math

import jax
import jax.numpy as jnp
from jax import lax
from jax.experimental import pallas as pl
from jax.experimental.pallas import tpu as pltpu
from jax.sharding import Mesh, PartitionSpec as P

AXES = ("z", "x", "y", "c")
CAP = 2
OWNERS = 16
HD = 128
GROUPS = 8
KV_HALF = 4
HEADS_HALF = 32
HALF = HEADS_HALF * HD
WIDE = HALF + HD
BLOCK = 2048
CHIP_SPAN = 2 * BLOCK
MASKED = -1e30
SCALE = math.log2(math.e) / math.sqrt(HD)
NT = (((1,), (1,)), ((), ()))
F32 = jnp.float32
BF16 = jnp.bfloat16


def lanes(shape):
    return lax.broadcasted_iota(jnp.int32, shape, len(shape) - 1)


def split_three(value, lane):
    high = value.astype(BF16).astype(F32)
    rest = value - high
    middle = rest.astype(BF16).astype(F32)
    low = rest - middle
    return jnp.where(lane < 32, high, jnp.where(lane < 64, middle, low)).astype(BF16)


def join_three(block):
    wide = block.astype(F32)
    return wide + pltpu.roll(wide, 96, 1) + pltpu.roll(wide, 64, 1)


def dispatch_kernel(ids, core_ref, q_ref, mine_ref, other_ref, pick_ref):
    core = core_ref[0]
    rows = q_ref.shape[0]
    row = lax.broadcasted_iota(jnp.int32, (OWNERS * CAP, rows), 0)
    column = lanes((OWNERS * CAP, rows))
    pick_row = lax.broadcasted_iota(jnp.int32, (rows, HD), 0)
    pick_lane = lanes((rows, HD))
    placing = jnp.zeros((OWNERS * CAP, rows), F32)
    pick = jnp.zeros((rows, HD), F32)
    for i in range(rows):
        slot = ids[i] * CAP
        for e in range(i):
            slot = slot + (ids[e] == ids[i]).astype(jnp.int32)
        placing = jnp.where((row == slot) & (column == i), 1.0, placing)
        pick = jnp.where((pick_lane == slot) & (pick_row == i), 1.0, pick)
    placing = placing.astype(BF16)
    pick_ref[...] = pick.astype(BF16)
    flags = jnp.ones((rows, HD), BF16)
    for target, half in ((mine_ref, core), (other_ref, 1 - core)):
        part = q_ref[:, pl.ds(pl.multiple_of(half * HALF, HALF), HALF)]
        target[:, :HALF] = jnp.dot(placing, part, preferred_element_type=F32).astype(BF16)
        target[:, HALF:] = jnp.dot(placing, flags, preferred_element_type=F32).astype(BF16)


def dispatch(queries, prefix_ids, core):
    rows = queries.shape[0]
    slots = OWNERS * CAP
    return pl.pallas_call(
        dispatch_kernel,
        in_specs=[
            pl.BlockSpec(memory_space=pltpu.SMEM),
            pl.BlockSpec(memory_space=pltpu.SMEM),
            pl.BlockSpec(memory_space=pltpu.VMEM),
        ],
        out_specs=[pl.BlockSpec(memory_space=pltpu.VMEM)] * 3,
        out_shape=[
            jax.ShapeDtypeStruct((slots, WIDE), BF16),
            jax.ShapeDtypeStruct((slots, WIDE), BF16),
            jax.ShapeDtypeStruct((rows, HD), BF16),
        ],
        name="dispatch",
    )(prefix_ids, core, queries)


def suffix_kernel(lengths, q_ref, k_ref, v_ref, o_ref, lse_ref):
    i = pl.program_id(0)
    length = lengths[i]
    span = k_ref.shape[2]
    kv_heads = k_ref.shape[1]
    heads = kv_heads * GROUPS
    scores = [
        lax.dot_general(
            q_ref[0, k * GROUPS : (k + 1) * GROUPS], k_ref[0, k], NT, preferred_element_type=F32
        )
        for k in range(kv_heads)
    ]
    scores = jnp.concatenate(scores, axis=0) * SCALE
    valid = lanes((heads, span)) < length
    scores = jnp.where(valid, scores, MASKED)
    peak = jnp.max(scores, axis=1, keepdims=True)
    weights = jnp.where(valid, jnp.exp2(scores - peak), 0.0)
    total = jnp.sum(weights, axis=1, keepdims=True)
    rounded = weights.astype(BF16)
    outs = [
        jnp.dot(rounded[k * GROUPS : (k + 1) * GROUPS], v_ref[0, k], preferred_element_type=F32)
        for k in range(kv_heads)
    ]
    out = jnp.concatenate(outs, axis=0) / total
    here = lax.broadcasted_iota(jnp.int32, lse_ref.shape, 0) == i
    for h in range(heads):
        place = slice(h * HD, (h + 1) * HD)
        o_ref[:, place] = jnp.where(here, out[h : h + 1], o_ref[:, place])
    lse = jnp.broadcast_to(peak + jnp.log2(total), (heads, HD))
    diagonal = lax.broadcasted_iota(jnp.int32, (heads, HD), 0) == lanes((heads, HD))
    row = jnp.sum(jnp.where(diagonal, lse, 0.0), axis=0, keepdims=True)
    lse_ref[...] = jnp.where(here, row, lse_ref[...])


def suffix(queries, keys, values, lengths):
    rows, kv_heads, span, hd = keys.shape
    heads = kv_heads * GROUPS
    return pl.pallas_call(
        suffix_kernel,
        grid_spec=pltpu.PrefetchScalarGridSpec(
            num_scalar_prefetch=1,
            grid=(rows,),
            in_specs=[
                pl.BlockSpec((1, heads, hd), lambda i, *_: (i, 0, 0)),
                pl.BlockSpec((1, kv_heads, span, hd), lambda i, *_: (i, 0, 0, 0)),
                pl.BlockSpec((1, kv_heads, span, hd), lambda i, *_: (i, 0, 0, 0)),
            ],
            out_specs=[
                pl.BlockSpec((rows, heads * hd), lambda i, *_: (0, 0)),
                pl.BlockSpec((rows, hd), lambda i, *_: (0, 0)),
            ],
        ),
        out_shape=[
            jax.ShapeDtypeStruct((rows, heads * hd), F32),
            jax.ShapeDtypeStruct((rows, hd), F32),
        ],
        compiler_params=pltpu.CompilerParams(vmem_limit_bytes=24 << 20),
        cost_estimate=pl.CostEstimate(
            flops=4 * rows * heads * span * hd,
            bytes_accessed=4 * rows * kv_heads * span * hd,
            transcendentals=rows * heads * span,
        ),
        name="suffix",
    )(lengths, queries.reshape(rows, heads, hd), keys, values)


def prefix_kernel(
    meta, x_ref, k_own, v_own, k_peer, v_peer, o_ref, keys, values, m_ref, lse_ref, sems
):
    length = meta[0]
    core = meta[1]
    count = x_ref.shape[0]
    rows = GROUPS * count
    sub = min(256, rows)
    own = pl.ds(pl.multiple_of(core * BLOCK, BLOCK), BLOCK)
    peer = pl.ds(pl.multiple_of((1 - core) * BLOCK, BLOCK), BLOCK)

    def copies(j):
        return (
            pltpu.make_async_copy(k_own.at[core * KV_HALF + j], keys.at[j, own], sems.at[j, 0]),
            pltpu.make_async_copy(k_peer.at[j], keys.at[j, peer], sems.at[j, 1]),
            pltpu.make_async_copy(v_own.at[core * KV_HALF + j], values.at[j, own], sems.at[j, 2]),
            pltpu.make_async_copy(v_peer.at[j], values.at[j, peer], sems.at[j, 3]),
        )

    for j in range(KV_HALF):
        for copy in copies(j):
            copy.start()

    def step(j, q, first, span, masked, accs):
        place = pl.ds(pl.multiple_of(first, span), span)
        key = keys[j, place, :]
        value = values[j, place, :]
        ones = jnp.ones((span, HD), BF16)
        if masked:
            inside = first + lax.broadcasted_iota(jnp.int32, (span, HD), 0) < length
            value = jnp.where(inside, value, jnp.zeros_like(value))
            ones = jnp.where(inside, ones, jnp.zeros_like(ones))
        value = jnp.concatenate([value, ones], axis=1)
        out = []
        for u in range(rows // sub):
            part = slice(u * sub, (u + 1) * sub)
            scores = lax.dot_general(q[part], key, NT, preferred_element_type=F32) * SCALE
            base = jnp.concatenate([m_ref[part, :]] * (span // HD), axis=1)
            weights = jnp.exp2(scores - base).astype(BF16)
            out.append(accs[u] + jnp.dot(weights, value, preferred_element_type=F32))
        return tuple(out)

    def head(j, _):
        for copy in copies(j):
            copy.wait()
        start = pl.multiple_of(j * GROUPS * HD, GROUPS * HD)
        q = jnp.concatenate(
            [x_ref[:, pl.ds(start + g * HD, HD)] for g in range(GROUPS)], axis=0
        )

        def peak_of(first):
            key = keys[j, pl.ds(pl.multiple_of(first, 256), 256), :]
            scores = lax.dot_general(q, key, NT, preferred_element_type=F32) * SCALE
            scores = jnp.where(first + lanes((rows, 256)) < length, scores, MASKED)
            return jnp.broadcast_to(jnp.max(scores, axis=1, keepdims=True), (rows, HD))

        m_ref[...] = peak_of(0)

        def attempt(state):
            turn = state[0]

            @pl.when(turn == 1)
            def _():
                def more(t, carry):
                    m_ref[...] = jnp.maximum(m_ref[...], peak_of(t * 256))
                    return carry

                lax.fori_loop(1, (length + 255) // 256, more, 0)

            accs = tuple(jnp.zeros((sub, 2 * HD), F32) for _ in range(rows // sub))
            whole = length // 2048
            accs = lax.fori_loop(
                0, whole, lambda t, a: step(j, q, t * 2048, 2048, False, a), accs
            )
            accs = lax.fori_loop(
                whole * 4,
                (length + 511) // 512,
                lambda t, a: step(j, q, t * 512, 512, True, a),
                accs,
            )
            acc = jnp.concatenate(accs, axis=0)
            total = acc[:, HD:]
            out = (acc[:, :HD] / total).astype(BF16)
            lse = m_ref[...] + jnp.log2(total)
            lane = lanes((count, HD)) % 32
            for g in range(GROUPS):
                part = slice(g * count, (g + 1) * count)
                o_ref[:, pl.ds(start + g * HD, HD)] = out[part]
                lse_ref[...] = jnp.where(lane == j * GROUPS + g, lse[part], lse_ref[...])
            wrong = jnp.sum(jnp.where(total < 1e30, 0.0, 1.0))
            return turn + 1, (wrong > 0.0).astype(jnp.int32)

        lax.while_loop(
            lambda state: (state[0] < 2) & (state[1] == 1), attempt, (jnp.int32(0), jnp.int32(1))
        )
        return 0

    @pl.when(length > 0)
    def _():
        lse_ref[...] = jnp.zeros_like(lse_ref)
        lax.fori_loop(0, KV_HALF, head, 0)

    @pl.when(length == 0)
    def _():
        for j in range(KV_HALF):
            for copy in copies(j):
                copy.wait()
        o_ref[:, :HALF] = jnp.zeros((count, HALF), BF16)
        lse_ref[...] = jnp.full_like(lse_ref, MASKED)

    o_ref[:, HALF:] = split_three(lse_ref[...], lanes((count, HD)))


def prefix_partial(x, meta, k_own, v_own, k_peer, v_peer):
    count = x.shape[0]
    any_space = pl.BlockSpec(memory_space=pl.ANY)
    return pl.pallas_call(
        prefix_kernel,
        in_specs=[
            pl.BlockSpec(memory_space=pltpu.SMEM),
            pl.BlockSpec(memory_space=pltpu.VMEM),
            any_space,
            any_space,
            any_space,
            any_space,
        ],
        out_specs=pl.BlockSpec(memory_space=pltpu.VMEM),
        out_shape=jax.ShapeDtypeStruct((count, WIDE), BF16),
        scratch_shapes=[
            pltpu.VMEM((KV_HALF, CHIP_SPAN, HD), BF16),
            pltpu.VMEM((KV_HALF, CHIP_SPAN, HD), BF16),
            pltpu.VMEM((GROUPS * count, HD), F32),
            pltpu.VMEM((count, HD), F32),
            pltpu.SemaphoreType.DMA((KV_HALF, 4)),
        ],
        compiler_params=pltpu.CompilerParams(vmem_limit_bytes=48 << 20),
        cost_estimate=pl.CostEstimate(
            flops=4 * 4 * count * HEADS_HALF * CHIP_SPAN * HD,
            bytes_accessed=16 * BLOCK * KV_HALF * HD,
            transcendentals=count * HEADS_HALF * CHIP_SPAN,
        ),
        name="prefix_partial",
    )(meta, x, k_own, v_own, k_peer, v_peer)


def merge_kernel(*refs):
    parts, out_ref = refs[:-1], refs[-1]
    sums = [join_three(part[:, HALF:]) for part in parts]
    top = functools.reduce(jnp.maximum, sums)
    shares = [jnp.exp2(s - top) for s in sums]
    whole = functools.reduce(jnp.add, shares)
    shares = [s / whole for s in shares]
    for h in range(HEADS_HALF):
        block = slice(h * HD, (h + 1) * HD)
        out = None
        for part, share in zip(parts, shares):
            term = part[:, block].astype(F32) * share[:, h : h + 1]
            out = term if out is None else out + term
        out_ref[:, block] = out.astype(BF16)
    lane = lanes(top.shape)
    lse = jnp.where(lane < 32, top + jnp.log2(whole), 0.0)
    lse = lse + pltpu.roll(lse, 32, 1) + pltpu.roll(lse, 64, 1)
    out_ref[:, HALF:] = split_three(lse, lane)


def merge(*parts):
    return pl.pallas_call(
        merge_kernel,
        out_shape=jax.ShapeDtypeStruct(parts[0].shape, BF16),
        name="merge",
    )(*parts)


def finish_kernel(core_ref, mine_ref, got_ref, pick_ref, o_ref, lse_ref, out_ref):
    core = core_ref[0]
    slots = mine_ref.shape[0]
    pick = pick_ref[:, :slots]
    mine = jnp.dot(pick, mine_ref[...], preferred_element_type=F32)
    got = jnp.dot(pick, got_ref[...], preferred_element_type=F32)
    lower = core == 0
    for half in range(2):
        own = lower if half == 0 else jnp.logical_not(lower)
        part = jnp.where(own, mine, got)
        prefix_lse = join_three(part[:, HALF:])
        suffix_lse = lse_ref[...]
        if half:
            suffix_lse = pltpu.roll(suffix_lse, 96, 1)
        top = jnp.maximum(prefix_lse, suffix_lse)
        prefix_share = jnp.exp2(prefix_lse - top)
        suffix_share = jnp.exp2(suffix_lse - top)
        whole = prefix_share + suffix_share
        prefix_share = prefix_share / whole
        suffix_share = suffix_share / whole
        for h in range(HEADS_HALF):
            block = slice(h * HD, (h + 1) * HD)
            place = slice(half * HALF + h * HD, half * HALF + (h + 1) * HD)
            out_ref[:, place] = (
                part[:, block] * prefix_share[:, h : h + 1]
                + o_ref[:, place] * suffix_share[:, h : h + 1]
            ).astype(BF16)


def finish(core, mine, got, pick, suffix_out, suffix_lse):
    space = pl.BlockSpec(memory_space=pltpu.VMEM)
    return pl.pallas_call(
        finish_kernel,
        in_specs=[pl.BlockSpec(memory_space=pltpu.SMEM)] + [space] * 5,
        out_specs=space,
        out_shape=jax.ShapeDtypeStruct(suffix_out.shape, BF16),
        name="finish",
    )(core, mine, got, pick, suffix_out, suffix_lse)


def ring(shift):
    return [(i, (i + shift) % 4) for i in range(4)]


SWAP = [(0, 1), (1, 0)]


def local(
    queries,
    prefix_ids,
    prefix_lengths,
    prefix_keys,
    prefix_values,
    suffix_keys,
    suffix_values,
    suffix_lengths,
):
    core = lax.axis_index("c")
    chip = lax.axis_index("y")
    core_array = core.reshape(1).astype(jnp.int32)
    keys = prefix_keys[0]
    values = prefix_values[0]
    k_peer = lax.ppermute(
        lax.dynamic_slice_in_dim(keys, (1 - core) * KV_HALF, KV_HALF, 0), "c", SWAP
    )
    v_peer = lax.ppermute(
        lax.dynamic_slice_in_dim(values, (1 - core) * KV_HALF, KV_HALF, 0), "c", SWAP
    )
    mine, other, pick = dispatch(queries, prefix_ids, core_array)
    got = lax.ppermute(other, "c", SWAP)
    leaving = jnp.concatenate(
        [mine.reshape(OWNERS, CAP, WIDE), got.reshape(OWNERS, CAP, WIDE)], axis=1
    )
    arrived = lax.all_to_all(leaving, ("z", "x"), split_axis=0, concat_axis=0, tiled=True)
    arrived = arrived.reshape(OWNERS * 2 * CAP, WIDE)
    suffix_out, suffix_lse = suffix(queries, suffix_keys, suffix_values, suffix_lengths)

    count = jnp.clip(prefix_lengths[0] - chip * CHIP_SPAN, 0, CHIP_SPAN)
    meta = jnp.stack([count, core]).astype(jnp.int32)
    work = functools.partial(
        prefix_partial, meta=meta, k_own=keys, v_own=values, k_peer=k_peer, v_peer=v_peer
    )
    from_left = lax.ppermute(arrived, "y", ring(1))
    from_right = lax.ppermute(arrived, "y", ring(3))
    from_far = lax.ppermute(arrived, "y", ring(2))
    size = arrived.shape[0]
    for_left = work(from_left)
    back_left = lax.ppermute(for_left, "y", ring(3))
    for_right = work(from_right)
    back_right = lax.ppermute(for_right, "y", ring(1))
    for_far = work(from_far)
    back_far = lax.ppermute(for_far, "y", ring(2))
    for_self = work(arrived)
    merged = merge(for_self, back_left, back_right, back_far)
    returned = lax.all_to_all(
        merged.reshape(OWNERS, 2 * CAP, WIDE), ("z", "x"), split_axis=0, concat_axis=0, tiled=True
    )
    mine_back = returned[:, :CAP].reshape(OWNERS * CAP, WIDE)
    got_back = lax.ppermute(returned[:, CAP:].reshape(OWNERS * CAP, WIDE), "c", SWAP)
    return finish(core_array, mine_back, got_back, pick, suffix_out, suffix_lse)


def solution(mesh):
    fine = Mesh(mesh.devices.reshape(4, 4, 4, 2), AXES)
    rows = P(AXES)
    placed = (
        P(AXES, None),
        rows,
        P(("z", "x")),
        P(("z", "x"), None, ("y", "c"), None),
        P(("z", "x"), None, ("y", "c"), None),
        P(AXES, None, None, None),
        P(AXES, None, None, None),
        rows,
    )
    return jax.shard_map(
        local, mesh=fine, in_specs=placed, out_specs=P(AXES, None), check_vma=False
    )
```

```python
import functools
import math

import jax
import jax.numpy as jnp
from jax import lax
from jax.experimental import pallas as pl
from jax.experimental.pallas import tpu as pltpu
from jax.sharding import Mesh, PartitionSpec as P

AXES = ("z", "x", "y", "c")
PLANE = ("z", "x", "c")
CAP = 2
OWNERS = 16
HD = 128
GROUPS = 8
KV_HALF = 4
HEADS_HALF = 32
HALF = HEADS_HALF * HD
WIDE = HALF + HD
BLOCK = 2048
PAD = 16
SUFFIX_STEP = 2
SMALL = 32
CHIP_SPAN = 2 * BLOCK
MASKED = -1e30
SCALE = math.log2(math.e) / math.sqrt(HD)
NT = (((1,), (1,)), ((), ()))
F32 = jnp.float32
BF16 = jnp.bfloat16


def lanes(shape):
    return lax.broadcasted_iota(jnp.int32, shape, len(shape) - 1)


def split_three(value, lane):
    high = value.astype(BF16).astype(F32)
    rest = value - high
    middle = rest.astype(BF16).astype(F32)
    low = rest - middle
    return jnp.where(lane < 32, high, jnp.where(lane < 64, middle, low)).astype(BF16)


def join_three(block):
    wide = block.astype(F32)
    return wide + pltpu.roll(wide, 96, 1) + pltpu.roll(wide, 64, 1)


def dispatch_kernel(ids, q_ref, out_ref, pick_ref):
    rows = q_ref.shape[0]
    slots = 2 * CAP * OWNERS
    row = lax.broadcasted_iota(jnp.int32, (slots, 2 * rows), 0)
    column = lanes((slots, 2 * rows))
    pick_row = lax.broadcasted_iota(jnp.int32, (2 * rows, HD), 0)
    pick_lane = lanes((2 * rows, HD))
    placing = jnp.zeros((slots, 2 * rows), F32)
    pick = jnp.zeros((2 * rows, HD), F32)
    for i in range(rows):
        slot = ids[i] * (2 * CAP)
        for e in range(i):
            slot = slot + (ids[e] == ids[i]).astype(jnp.int32)
        for half in range(2):
            place = slot + half * CAP
            entry = half * rows + i
            placing = jnp.where((row == place) & (column == entry), 1.0, placing)
            pick = jnp.where((pick_lane == place) & (pick_row == entry), 1.0, pick)
    placing = placing.astype(BF16)
    pick_ref[...] = pick.astype(BF16)
    wide = q_ref[...].astype(F32)
    halves = jnp.concatenate([wide[:, :HALF], wide[:, HALF:]], axis=0).astype(BF16)
    flags = jnp.ones((2 * rows, HD), BF16)
    out_ref[:, :HALF] = jnp.dot(placing, halves, preferred_element_type=F32).astype(BF16)
    out_ref[:, HALF:] = jnp.dot(placing, flags, preferred_element_type=F32).astype(BF16)


def dispatch(queries, prefix_ids):
    rows = queries.shape[0]
    return pl.pallas_call(
        dispatch_kernel,
        in_specs=[
            pl.BlockSpec(memory_space=pltpu.SMEM),
            pl.BlockSpec(memory_space=pltpu.VMEM),
        ],
        out_specs=[pl.BlockSpec(memory_space=pltpu.VMEM)] * 2,
        out_shape=[
            jax.ShapeDtypeStruct((2 * CAP * OWNERS, WIDE), BF16),
            jax.ShapeDtypeStruct((2 * rows, HD), BF16),
        ],
        name="dispatch",
    )(prefix_ids, queries)


def suffix_kernel(lengths, q_ref, k_hbm, v_hbm, o_ref, lse_ref, k_ref, v_ref, sems):
    count, kv_heads, span, _ = k_ref.shape
    block = q_ref.shape[0]
    heads = kv_heads * GROUPS
    upper = lax.broadcasted_iota(jnp.int32, (2 * GROUPS, 2 * HD), 0) < GROUPS
    left = lanes((2 * GROUPS, 2 * HD)) < HD
    diagonal = lax.broadcasted_iota(jnp.int32, (heads, HD), 0) == lanes((heads, HD))

    def copies(i):
        parts = [slice(0, kv_heads // 2), slice(kv_heads // 2, kv_heads)]
        return [
            pltpu.make_async_copy(hbm.at[i, part], ref.at[i, part], sems.at[i, 2 * a + b])
            for a, (hbm, ref) in enumerate(((k_hbm, k_ref), (v_hbm, v_ref)))
            for b, part in enumerate(parts)
        ]

    @pl.when(pl.program_id(0) == 0)
    def _():
        for i in range(count):
            for copy in copies(i):
                copy.start()

    def pair(ref, i, k):
        return jnp.concatenate([ref[i, k], ref[i, k + 1]], axis=1)

    for e in range(block):
        i = pl.program_id(0) * block + e
        length = lengths[i]
        for copy in copies(i):
            copy.wait()
        scores = []
        for k in range(0, kv_heads, 2):
            q = q_ref[e, k * GROUPS : (k + 2) * GROUPS]
            q = jnp.where(upper == left, jnp.concatenate([q, q], axis=1), 0.0).astype(BF16)
            scores.append(lax.dot_general(q, pair(k_ref, i, k), NT, preferred_element_type=F32))
        scores = jnp.concatenate(scores, axis=0) * SCALE
        valid = lanes((heads, span)) < length
        scores = jnp.where(valid, scores, MASKED)
        peak = jnp.max(scores, axis=1, keepdims=True)
        weights = jnp.where(valid, jnp.exp2(scores - peak), 0.0)
        total = jnp.sum(weights, axis=1, keepdims=True)
        rounded = weights.astype(BF16)
        outs = []
        for k in range(0, kv_heads, 2):
            part = rounded[k * GROUPS : (k + 2) * GROUPS]
            both = jnp.dot(part, pair(v_ref, i, k), preferred_element_type=F32)
            outs += [both[:GROUPS, :HD], both[GROUPS:, HD:]]
        out = jnp.concatenate(outs, axis=0) / total
        here = lax.broadcasted_iota(jnp.int32, lse_ref.shape, 0) == i
        for h in range(heads):
            place = slice(h * HD, (h + 1) * HD)
            o_ref[:, place] = jnp.where(here, out[h : h + 1], o_ref[:, place])
        lse = jnp.broadcast_to(peak + jnp.log2(total), (heads, HD))
        row = jnp.sum(jnp.where(diagonal, lse, 0.0), axis=0, keepdims=True)
        lse_ref[...] = jnp.where(here, row, lse_ref[...])


def suffix(queries, keys, values, lengths):
    rows, kv_heads, span, hd = keys.shape
    heads = kv_heads * GROUPS
    return pl.pallas_call(
        suffix_kernel,
        grid_spec=pltpu.PrefetchScalarGridSpec(
            num_scalar_prefetch=1,
            grid=(rows // SUFFIX_STEP,),
            in_specs=[
                pl.BlockSpec((SUFFIX_STEP, heads, hd), lambda i, *_: (i, 0, 0)),
                pl.BlockSpec(memory_space=pl.ANY),
                pl.BlockSpec(memory_space=pl.ANY),
            ],
            out_specs=[
                pl.BlockSpec((rows, heads * hd), lambda i, *_: (0, 0)),
                pl.BlockSpec((rows, hd), lambda i, *_: (0, 0)),
            ],
            scratch_shapes=[
                pltpu.VMEM((rows, kv_heads, span, hd), BF16),
                pltpu.VMEM((rows, kv_heads, span, hd), BF16),
                pltpu.SemaphoreType.DMA((rows, 4)),
            ],
        ),
        out_shape=[
            jax.ShapeDtypeStruct((rows, heads * hd), F32),
            jax.ShapeDtypeStruct((rows, hd), F32),
        ],
        compiler_params=pltpu.CompilerParams(vmem_limit_bytes=56 << 20),
        cost_estimate=pl.CostEstimate(
            flops=4 * rows * heads * span * hd,
            bytes_accessed=4 * rows * kv_heads * span * hd,
            transcendentals=rows * heads * span,
        ),
        name="suffix",
    )(lengths, queries.reshape(rows, heads, hd), keys, values)


def prepare_kernel(core_ref, k_ref, v_ref, own_ref, other_ref, k_other):
    core = core_ref[0]
    k_other[...] = k_ref[...]
    rows = lax.broadcasted_iota(jnp.int32, (HD, HD), 0)
    unit = (rows == lanes((HD, HD))).astype(BF16)
    for half, out_ref in ((core, own_ref), (1 - core, other_ref)):
        turned = lax.dot_general(unit, v_ref[half, 0], NT, preferred_element_type=F32)
        out_ref[0] = turned.astype(BF16)


def prepare(core, keys, values):
    turned = jax.ShapeDtypeStruct((KV_HALF, HD, BLOCK), BF16)
    return pl.pallas_call(
        prepare_kernel,
        grid_spec=pltpu.PrefetchScalarGridSpec(
            num_scalar_prefetch=1,
            grid=(KV_HALF,),
            in_specs=[
                pl.BlockSpec((1, BLOCK, HD), lambda j, c: ((1 - c[0]) * KV_HALF + j, 0, 0)),
                pl.BlockSpec((2, 1, BLOCK, HD), lambda j, c: (0, j, 0, 0)),
            ],
            out_specs=[
                pl.BlockSpec((1, HD, BLOCK), lambda j, c: (j, 0, 0)),
                pl.BlockSpec((1, HD, BLOCK), lambda j, c: (j, 0, 0)),
                pl.BlockSpec((1, BLOCK, HD), lambda j, c: (j, 0, 0)),
            ],
        ),
        out_shape=[turned, turned, jax.ShapeDtypeStruct((KV_HALF, BLOCK, HD), BF16)],
        compiler_params=pltpu.CompilerParams(vmem_limit_bytes=56 << 20),
        cost_estimate=pl.CostEstimate(
            flops=4 * HD * HD * KV_HALF * BLOCK,
            bytes_accessed=12 * BLOCK * KV_HALF * HD,
            transcendentals=0,
        ),
        name="prepare",
    )(core, keys, values.reshape(2, KV_HALF, BLOCK, HD))


def prefix_kernel(meta, *refs, groups):
    x_refs, refs = refs[:groups], refs[groups:]
    (k_own, k_peer, v_own, v_peer), refs = refs[:4], refs[4:]
    o_refs, refs = refs[:groups], refs[groups:]
    keys, turned, m_ref, lse_ref, small_x, small_o, sems = refs
    length = meta[0]
    core = meta[1]
    slots = x_refs[0].shape[0]
    own = pl.ds(pl.multiple_of(core * BLOCK, BLOCK), BLOCK)
    peer = pl.ds(pl.multiple_of((1 - core) * BLOCK, BLOCK), BLOCK)

    def copies(j):
        return (
            pltpu.make_async_copy(k_own.at[core * KV_HALF + j], keys.at[j, own], sems.at[j, 0]),
            pltpu.make_async_copy(k_peer.at[j], keys.at[j, peer], sems.at[j, 1]),
            pltpu.make_async_copy(v_own.at[j], turned.at[j, :HD, own], sems.at[j, 2]),
            pltpu.make_async_copy(v_peer.at[j], turned.at[j, :HD, peer], sems.at[j, 3]),
        )

    def attend(sources, targets, count):
        rows = groups * GROUPS * count

        def step(j, q, first, span, masked, acc):
            place = pl.ds(pl.multiple_of(first, span), span)
            scores = lax.dot_general(keys[j, place, :], q, NT, preferred_element_type=F32) * SCALE
            weights = jnp.exp2(scores - m_ref[0:1, :rows])
            if masked:
                inside = first + lax.broadcasted_iota(jnp.int32, weights.shape, 0) < length
                weights = jnp.where(inside, weights, 0.0)
            value = turned[j, :, place]
            return acc + jnp.dot(value, weights.astype(BF16), preferred_element_type=F32)

        def head(j, _):
            @pl.when(j < KV_HALF - 1)
            def _():
                for copy in copies(j + 1):
                    copy.start()

            for copy in copies(j):
                copy.wait()
            start = pl.multiple_of(j * GROUPS * HD, GROUPS * HD)
            q = jnp.concatenate(
                [x[:, pl.ds(start + g * HD, HD)] for x in sources for g in range(GROUPS)], axis=0
            )

            def peak_of(first):
                key = keys[j, pl.ds(pl.multiple_of(first, 256), 256), :]
                scores = lax.dot_general(key, q, NT, preferred_element_type=F32) * SCALE
                inside = first + lax.broadcasted_iota(jnp.int32, scores.shape, 0) < length
                peak = jnp.max(jnp.where(inside, scores, MASKED), axis=0, keepdims=True)
                return jnp.broadcast_to(peak, (8, rows))

            m_ref[:, :rows] = peak_of(0)

            def attempt(state):
                turn = state[0]

                @pl.when(turn == 1)
                def _():
                    def more(t, carry):
                        m_ref[:, :rows] = jnp.maximum(m_ref[:, :rows], peak_of(t * 256))
                        return carry

                    lax.fori_loop(1, (length + 255) // 256, more, 0)

                def full(acc):
                    return step(j, q, 0, CHIP_SPAN, False, acc)

                def partial(acc):
                    first = jnp.int32(0)
                    for span in (2048, 1024):
                        fits = length - first >= span
                        acc = lax.cond(
                            fits,
                            functools.partial(step, j, q, first, span, False),
                            lambda a: a,
                            acc,
                        )
                        first = first + jnp.where(fits, span, 0)
                    return lax.fori_loop(
                        first // 512,
                        (length + 511) // 512,
                        lambda t, a: step(j, q, t * 512, 512, True, a),
                        acc,
                    )

                acc = jnp.zeros((HD + PAD, rows), F32)
                acc = lax.cond(length == CHIP_SPAN, full, partial, acc)
                total = acc[HD : HD + 1]
                out = (acc[:HD] / total).T.astype(BF16)
                lse = jnp.broadcast_to(m_ref[0:1, :rows] + jnp.log2(total), (HD, rows)).T
                lane = lanes((count, HD)) % 32
                for i in range(groups):
                    for g in range(GROUPS):
                        part = slice((i * GROUPS + g) * count, (i * GROUPS + g + 1) * count)
                        targets[i][:, pl.ds(start + g * HD, HD)] = out[part]
                        lse_ref[i, :count] = jnp.where(
                            lane == j * GROUPS + g, lse[part], lse_ref[i, :count]
                        )
                wrong = jnp.sum(jnp.where(total < 1e30, 0.0, 1.0))
                return turn + 1, (wrong > 0.0).astype(jnp.int32)

            lax.while_loop(
                lambda state: (state[0] < 2) & (state[1] == 1),
                attempt,
                (jnp.int32(0), jnp.int32(1)),
            )
            return 0

        lax.fori_loop(0, KV_HALF, head, 0)

    for copy in copies(0):
        copy.start()
    for j in range(KV_HALF):
        turned[j, HD:, :] = jnp.ones((PAD, CHIP_SPAN), BF16)
    lse_ref[...] = jnp.zeros_like(lse_ref)
    flags = [x[:, HALF:] for x in x_refs]
    few = functools.reduce(
        jnp.logical_and, [jnp.sum(flag.astype(F32)) <= SMALL * HD for flag in flags]
    )

    @pl.when((length > 0) & few)
    def _():
        earlier = lanes((slots, slots)) < lax.broadcasted_iota(jnp.int32, (slots, slots), 0)
        places = []
        for i in range(groups):
            rank = jnp.dot(earlier.astype(BF16), flags[i], preferred_element_type=F32)
            here = (rank.astype(jnp.int32) == lanes(rank.shape)) & (flags[i].astype(F32) > 0.5)
            place = here.astype(F32).astype(BF16)[:, :SMALL]
            places.append(place)
            small_x[i] = lax.dot_general(
                place,
                x_refs[i][:, :HALF],
                (((0,), (0,)), ((), ())),
                preferred_element_type=F32,
            ).astype(BF16)
        attend(
            [small_x.at[i] for i in range(groups)], [small_o.at[i] for i in range(groups)], SMALL
        )
        for i in range(groups):
            o_refs[i][:, :HALF] = jnp.dot(
                places[i], small_o[i], preferred_element_type=F32
            ).astype(BF16)
            lse = split_three(lse_ref[i, :SMALL], lanes((SMALL, HD)))
            o_refs[i][:, HALF:] = jnp.dot(places[i], lse, preferred_element_type=F32).astype(BF16)

    @pl.when((length > 0) & jnp.logical_not(few))
    def _():
        attend(x_refs, o_refs, slots)
        for i in range(groups):
            o_refs[i][:, HALF:] = split_three(lse_ref[i], lanes((slots, HD)))

    @pl.when(length == 0)
    def _():
        for copy in copies(0):
            copy.wait()
        for o_ref in o_refs:
            o_ref[:, :HALF] = jnp.zeros((slots, HALF), BF16)
            o_ref[:, HALF:] = split_three(
                jnp.full((slots, HD), MASKED, F32), lanes((slots, HD))
            )


def prefix_partial(xs, meta, k_own, k_peer, v_own, v_peer):
    groups = len(xs)
    count = xs[0].shape[0]
    inside = pl.BlockSpec(memory_space=pltpu.VMEM)
    return pl.pallas_call(
        functools.partial(prefix_kernel, groups=groups),
        in_specs=[pl.BlockSpec(memory_space=pltpu.SMEM)]
        + [inside] * groups
        + [pl.BlockSpec(memory_space=pl.ANY)] * 4,
        out_specs=[inside] * groups,
        out_shape=[jax.ShapeDtypeStruct((count, WIDE), BF16)] * groups,
        scratch_shapes=[
            pltpu.VMEM((KV_HALF, CHIP_SPAN, HD), BF16),
            pltpu.VMEM((KV_HALF, HD + PAD, CHIP_SPAN), BF16),
            pltpu.VMEM((8, groups * GROUPS * count), F32),
            pltpu.VMEM((groups, count, HD), F32),
            pltpu.VMEM((groups, SMALL, HALF), BF16),
            pltpu.VMEM((groups, SMALL, HALF), BF16),
            pltpu.SemaphoreType.DMA((KV_HALF, 4)),
        ],
        compiler_params=pltpu.CompilerParams(vmem_limit_bytes=56 << 20),
        cost_estimate=pl.CostEstimate(
            flops=16 * groups * count * HEADS_HALF * CHIP_SPAN * HD,
            bytes_accessed=16 * BLOCK * KV_HALF * HD,
            transcendentals=groups * count * HEADS_HALF * CHIP_SPAN,
        ),
        name="prefix_partial",
    )(meta, *xs, k_own, k_peer, v_own, v_peer)


def merge_kernel(*refs):
    parts, out_ref = refs[:-1], refs[-1]
    sums = [join_three(part[:, HALF:]) for part in parts]
    top = functools.reduce(jnp.maximum, sums)
    shares = [jnp.exp2(s - top) for s in sums]
    whole = functools.reduce(jnp.add, shares)
    shares = [s / whole for s in shares]
    for h in range(HEADS_HALF):
        block = slice(h * HD, (h + 1) * HD)
        out = None
        for part, share in zip(parts, shares):
            term = part[:, block].astype(F32) * share[:, h : h + 1]
            out = term if out is None else out + term
        out_ref[:, block] = out.astype(BF16)
    lane = lanes(top.shape)
    lse = jnp.where(lane < 32, top + jnp.log2(whole), 0.0)
    lse = lse + pltpu.roll(lse, 32, 1) + pltpu.roll(lse, 64, 1)
    out_ref[:, HALF:] = split_three(lse, lane)


def merge(*parts):
    return pl.pallas_call(
        merge_kernel,
        out_shape=jax.ShapeDtypeStruct(parts[0].shape, BF16),
        name="merge",
    )(*parts)


def finish_kernel(back_ref, pick_ref, o_ref, lse_ref, out_ref):
    slots = back_ref.shape[0]
    rows = o_ref.shape[0]
    picked = jnp.dot(pick_ref[:, :slots], back_ref[...], preferred_element_type=F32)
    for half in range(2):
        part = picked[half * rows : (half + 1) * rows]
        prefix_lse = join_three(part[:, HALF:])
        suffix_lse = lse_ref[...]
        if half:
            suffix_lse = pltpu.roll(suffix_lse, 96, 1)
        top = jnp.maximum(prefix_lse, suffix_lse)
        prefix_share = jnp.exp2(prefix_lse - top)
        suffix_share = jnp.exp2(suffix_lse - top)
        whole = prefix_share + suffix_share
        prefix_share = prefix_share / whole
        suffix_share = suffix_share / whole
        for h in range(HEADS_HALF):
            block = slice(h * HD, (h + 1) * HD)
            place = slice(half * HALF + h * HD, half * HALF + (h + 1) * HD)
            out_ref[:, place] = (
                part[:, block] * prefix_share[:, h : h + 1]
                + o_ref[:, place] * suffix_share[:, h : h + 1]
            ).astype(BF16)


def finish(back, pick, suffix_out, suffix_lse):
    return pl.pallas_call(
        finish_kernel,
        out_shape=jax.ShapeDtypeStruct(suffix_out.shape, BF16),
        name="finish",
    )(back, pick, suffix_out, suffix_lse)


def ring(shift):
    return [(i, (i + shift) % 4) for i in range(4)]


SWAP = [(0, 1), (1, 0)]


def local(
    queries,
    prefix_ids,
    prefix_lengths,
    prefix_keys,
    prefix_values,
    suffix_keys,
    suffix_values,
    suffix_lengths,
):
    core = lax.axis_index("c")
    chip = lax.axis_index("y")
    keys = prefix_keys[0]
    values = prefix_values[0]
    slots = 2 * CAP * OWNERS
    leaving, pick = dispatch(queries, prefix_ids)
    v_own, v_other, k_other = prepare(core.reshape(1).astype(jnp.int32), keys, values)
    arrived = lax.all_to_all(
        leaving.reshape(2 * OWNERS, CAP, WIDE), PLANE, split_axis=0, concat_axis=0, tiled=True
    ).reshape(slots, WIDE)
    arrived, late, v_other, k_other = lax.optimization_barrier(
        (arrived, queries, v_other, k_other)
    )
    v_peer = lax.ppermute(v_other, "c", SWAP)
    k_peer = lax.ppermute(k_other, "c", SWAP)
    from_left = lax.ppermute(arrived, "y", ring(1))
    from_right = lax.ppermute(arrived, "y", ring(3))
    suffix_out, suffix_lse = suffix(late, suffix_keys, suffix_values, suffix_lengths)
    from_left, from_right, suffix_out, suffix_lse, far = lax.optimization_barrier(
        (from_left, from_right, suffix_out, suffix_lse, arrived)
    )
    from_far = lax.ppermute(far, "y", ring(2))

    count = jnp.clip(prefix_lengths[0] - chip * CHIP_SPAN, 0, CHIP_SPAN)
    meta = jnp.stack([count, core]).astype(jnp.int32)
    work = functools.partial(
        prefix_partial, meta=meta, k_own=keys, k_peer=k_peer, v_own=v_own, v_peer=v_peer
    )
    for_left, for_right = work([from_left, from_right])
    back_left = lax.ppermute(for_left, "y", ring(3))
    back_right = lax.ppermute(for_right, "y", ring(1))
    (for_far,) = work([from_far])
    back_far = lax.ppermute(for_far, "y", ring(2))
    (for_self,) = work([arrived])
    merged = merge(for_self, back_left, back_right, back_far)
    back = lax.all_to_all(
        merged.reshape(2 * OWNERS, CAP, WIDE), PLANE, split_axis=0, concat_axis=0, tiled=True
    ).reshape(slots, WIDE)
    return finish(back, pick, suffix_out, suffix_lse)


def solution(mesh):
    fine = Mesh(mesh.devices.reshape(4, 4, 4, 2), AXES)
    rows = P(AXES)
    placed = (
        P(AXES, None),
        rows,
        P(("z", "x")),
        P(("z", "x"), None, ("y", "c"), None),
        P(("z", "x"), None, ("y", "c"), None),
        P(AXES, None, None, None),
        P(AXES, None, None, None),
        rows,
    )
    return jax.shard_map(
        local, mesh=fine, in_specs=placed, out_specs=P(AXES, None), check_vma=False
    )
```

```python
import functools
import math

import jax
import jax.numpy as jnp
from jax import lax
from jax.experimental import pallas as pl
from jax.experimental.pallas import tpu as pltpu
from jax.sharding import Mesh, PartitionSpec as P

AXES = ("z", "x", "y", "c")
PLANE = ("z", "x", "c")
CAP = 2
OWNERS = 16
HD = 128
GROUPS = 8
KV_HALF = 4
HEADS_HALF = 32
HALF = HEADS_HALF * HD
WIDE = HALF + HD
BLOCK = 2048
PAD = 16
SUFFIX_STEP = 2
SMALL = 32
STRIDE = 1024
CHIP_SPAN = 2 * BLOCK
MASKED = -1e30
SCALE = math.log2(math.e) / math.sqrt(HD)
NT = (((1,), (1,)), ((), ()))
F32 = jnp.float32
BF16 = jnp.bfloat16


def lanes(shape):
    return lax.broadcasted_iota(jnp.int32, shape, len(shape) - 1)


def split_three(value, lane):
    high = value.astype(BF16).astype(F32)
    rest = value - high
    middle = rest.astype(BF16).astype(F32)
    low = rest - middle
    return jnp.where(lane < 32, high, jnp.where(lane < 64, middle, low)).astype(BF16)


def join_three(block):
    wide = block.astype(F32)
    return wide + pltpu.roll(wide, 96, 1) + pltpu.roll(wide, 64, 1)


def dispatch_kernel(ids, q_ref, out_ref, pick_ref):
    rows = q_ref.shape[0]
    slots = 2 * CAP * OWNERS
    row = lax.broadcasted_iota(jnp.int32, (slots, 2 * rows), 0)
    column = lanes((slots, 2 * rows))
    pick_row = lax.broadcasted_iota(jnp.int32, (2 * rows, HD), 0)
    pick_lane = lanes((2 * rows, HD))
    placing = jnp.zeros((slots, 2 * rows), F32)
    pick = jnp.zeros((2 * rows, HD), F32)
    for i in range(rows):
        slot = ids[i] * (2 * CAP)
        for e in range(i):
            slot = slot + (ids[e] == ids[i]).astype(jnp.int32)
        for half in range(2):
            place = slot + half * CAP
            entry = half * rows + i
            placing = jnp.where((row == place) & (column == entry), 1.0, placing)
            pick = jnp.where((pick_lane == place) & (pick_row == entry), 1.0, pick)
    placing = placing.astype(BF16)
    pick_ref[...] = pick.astype(BF16)
    wide = q_ref[...].astype(F32)
    halves = jnp.concatenate([wide[:, :HALF], wide[:, HALF:]], axis=0).astype(BF16)
    flags = jnp.ones((2 * rows, HD), BF16)
    out_ref[:, :HALF] = jnp.dot(placing, halves, preferred_element_type=F32).astype(BF16)
    out_ref[:, HALF:] = jnp.dot(placing, flags, preferred_element_type=F32).astype(BF16)


def dispatch(queries, prefix_ids):
    rows = queries.shape[0]
    return pl.pallas_call(
        dispatch_kernel,
        in_specs=[
            pl.BlockSpec(memory_space=pltpu.SMEM),
            pl.BlockSpec(memory_space=pltpu.VMEM),
        ],
        out_specs=[pl.BlockSpec(memory_space=pltpu.VMEM)] * 2,
        out_shape=[
            jax.ShapeDtypeStruct((2 * CAP * OWNERS, WIDE), BF16),
            jax.ShapeDtypeStruct((2 * rows, HD), BF16),
        ],
        name="dispatch",
    )(prefix_ids, queries)


def suffix_kernel(lengths, q_ref, k_hbm, v_hbm, o_ref, lse_ref, k_ref, v_ref, sems):
    count, kv_heads, span, _ = k_ref.shape
    block = q_ref.shape[0]
    heads = kv_heads * GROUPS
    upper = lax.broadcasted_iota(jnp.int32, (2 * GROUPS, 2 * HD), 0) < GROUPS
    left = lanes((2 * GROUPS, 2 * HD)) < HD
    diagonal = lax.broadcasted_iota(jnp.int32, (heads, HD), 0) == lanes((heads, HD))

    def copies(i):
        parts = [slice(0, kv_heads // 2), slice(kv_heads // 2, kv_heads)]
        return [
            pltpu.make_async_copy(hbm.at[i, part], ref.at[i, part], sems.at[i, 2 * a + b])
            for a, (hbm, ref) in enumerate(((k_hbm, k_ref), (v_hbm, v_ref)))
            for b, part in enumerate(parts)
        ]

    @pl.when(pl.program_id(0) == 0)
    def _():
        for i in range(count):
            for copy in copies(i):
                copy.start()

    def pair(ref, i, k):
        return jnp.concatenate([ref[i, k], ref[i, k + 1]], axis=1)

    for e in range(block):
        i = pl.program_id(0) * block + e
        length = lengths[i]
        for copy in copies(i):
            copy.wait()
        scores = []
        for k in range(0, kv_heads, 2):
            q = q_ref[e, k * GROUPS : (k + 2) * GROUPS]
            q = jnp.where(upper == left, jnp.concatenate([q, q], axis=1), 0.0).astype(BF16)
            scores.append(lax.dot_general(q, pair(k_ref, i, k), NT, preferred_element_type=F32))
        scores = jnp.concatenate(scores, axis=0) * SCALE
        valid = lanes((heads, span)) < length
        scores = jnp.where(valid, scores, MASKED)
        peak = jnp.max(scores, axis=1, keepdims=True)
        weights = jnp.where(valid, jnp.exp2(scores - peak), 0.0)
        total = jnp.sum(weights, axis=1, keepdims=True)
        rounded = weights.astype(BF16)
        outs = []
        for k in range(0, kv_heads, 2):
            part = rounded[k * GROUPS : (k + 2) * GROUPS]
            both = jnp.dot(part, pair(v_ref, i, k), preferred_element_type=F32)
            outs += [both[:GROUPS, :HD], both[GROUPS:, HD:]]
        out = jnp.concatenate(outs, axis=0) / total
        here = lax.broadcasted_iota(jnp.int32, lse_ref.shape, 0) == i
        for h in range(heads):
            place = slice(h * HD, (h + 1) * HD)
            o_ref[:, place] = jnp.where(here, out[h : h + 1], o_ref[:, place])
        lse = jnp.broadcast_to(peak + jnp.log2(total), (heads, HD))
        row = jnp.sum(jnp.where(diagonal, lse, 0.0), axis=0, keepdims=True)
        lse_ref[...] = jnp.where(here, row, lse_ref[...])


def suffix(queries, keys, values, lengths):
    rows, kv_heads, span, hd = keys.shape
    heads = kv_heads * GROUPS
    return pl.pallas_call(
        suffix_kernel,
        grid_spec=pltpu.PrefetchScalarGridSpec(
            num_scalar_prefetch=1,
            grid=(rows // SUFFIX_STEP,),
            in_specs=[
                pl.BlockSpec((SUFFIX_STEP, heads, hd), lambda i, *_: (i, 0, 0)),
                pl.BlockSpec(memory_space=pl.ANY),
                pl.BlockSpec(memory_space=pl.ANY),
            ],
            out_specs=[
                pl.BlockSpec((rows, heads * hd), lambda i, *_: (0, 0)),
                pl.BlockSpec((rows, hd), lambda i, *_: (0, 0)),
            ],
            scratch_shapes=[
                pltpu.VMEM((rows, kv_heads, span, hd), BF16),
                pltpu.VMEM((rows, kv_heads, span, hd), BF16),
                pltpu.SemaphoreType.DMA((rows, 4)),
            ],
        ),
        out_shape=[
            jax.ShapeDtypeStruct((rows, heads * hd), F32),
            jax.ShapeDtypeStruct((rows, hd), F32),
        ],
        compiler_params=pltpu.CompilerParams(vmem_limit_bytes=56 << 20),
        cost_estimate=pl.CostEstimate(
            flops=4 * rows * heads * span * hd,
            bytes_accessed=4 * rows * kv_heads * span * hd,
            transcendentals=rows * heads * span,
        ),
        name="suffix",
    )(lengths, queries.reshape(rows, heads, hd), keys, values)


def prepare_kernel(core_ref, k_ref, v_ref, own_ref, other_ref, k_other):
    core = core_ref[0]
    k_other[...] = k_ref[...]
    rows = lax.broadcasted_iota(jnp.int32, (HD, HD), 0)
    unit = (rows == lanes((HD, HD))).astype(BF16)
    for half, out_ref in ((core, own_ref), (1 - core, other_ref)):
        turned = lax.dot_general(unit, v_ref[half, 0], NT, preferred_element_type=F32)
        out_ref[0] = turned.astype(BF16)


def prepare(core, keys, values):
    turned = jax.ShapeDtypeStruct((KV_HALF, HD, BLOCK), BF16)
    return pl.pallas_call(
        prepare_kernel,
        grid_spec=pltpu.PrefetchScalarGridSpec(
            num_scalar_prefetch=1,
            grid=(KV_HALF,),
            in_specs=[
                pl.BlockSpec((1, BLOCK, HD), lambda j, c: ((1 - c[0]) * KV_HALF + j, 0, 0)),
                pl.BlockSpec((2, 1, BLOCK, HD), lambda j, c: (0, j, 0, 0)),
            ],
            out_specs=[
                pl.BlockSpec((1, HD, BLOCK), lambda j, c: (j, 0, 0)),
                pl.BlockSpec((1, HD, BLOCK), lambda j, c: (j, 0, 0)),
                pl.BlockSpec((1, BLOCK, HD), lambda j, c: (j, 0, 0)),
            ],
        ),
        out_shape=[turned, turned, jax.ShapeDtypeStruct((KV_HALF, BLOCK, HD), BF16)],
        compiler_params=pltpu.CompilerParams(vmem_limit_bytes=56 << 20),
        cost_estimate=pl.CostEstimate(
            flops=4 * HD * HD * KV_HALF * BLOCK,
            bytes_accessed=12 * BLOCK * KV_HALF * HD,
            transcendentals=0,
        ),
        name="prepare",
    )(core, keys, values.reshape(2, KV_HALF, BLOCK, HD))


def prefix_kernel(meta, *refs, groups):
    x_refs, refs = refs[:groups], refs[groups:]
    (k_own, k_peer, v_own, v_peer), refs = refs[:4], refs[4:]
    o_refs, refs = refs[:groups], refs[groups:]
    keys, turned, m_ref, lse_ref, small_x, small_o, sems = refs
    length = meta[0]
    core = meta[1]
    slots = x_refs[0].shape[0]
    own = pl.ds(pl.multiple_of(core * BLOCK, BLOCK), BLOCK)
    peer = pl.ds(pl.multiple_of((1 - core) * BLOCK, BLOCK), BLOCK)

    def copies(j):
        return (
            pltpu.make_async_copy(k_own.at[core * KV_HALF + j], keys.at[j, own], sems.at[j, 0]),
            pltpu.make_async_copy(k_peer.at[j], keys.at[j, peer], sems.at[j, 1]),
            pltpu.make_async_copy(v_own.at[j], turned.at[j, :HD, own], sems.at[j, 2]),
            pltpu.make_async_copy(v_peer.at[j], turned.at[j, :HD, peer], sems.at[j, 3]),
        )

    def attend(sources, targets, count):
        rows = groups * GROUPS * count

        def step(j, q, first, span, masked, acc):
            place = pl.ds(pl.multiple_of(first, span), span)
            scores = lax.dot_general(keys[j, place, :], q, NT, preferred_element_type=F32) * SCALE
            weights = jnp.exp2(scores - m_ref[0:1, :rows])
            if masked:
                inside = first + lax.broadcasted_iota(jnp.int32, weights.shape, 0) < length
                weights = jnp.where(inside, weights, 0.0)
            value = turned[j, :, place]
            return acc + jnp.dot(value, weights.astype(BF16), preferred_element_type=F32)

        def whole(j, q, span):
            scores = lax.dot_general(keys[j, :span], q, NT, preferred_element_type=F32) * SCALE
            weights = jnp.exp2(scores - m_ref[0:1, :rows])
            sure = span - STRIDE
            last = weights[sure:]
            inside = sure + lax.broadcasted_iota(jnp.int32, last.shape, 0) < length
            last = jnp.where(inside, last, 0.0).astype(BF16)
            if sure:
                last = jnp.concatenate([weights[:sure].astype(BF16), last], axis=0)
            return jnp.dot(turned[j, :, :span], last, preferred_element_type=F32)

        def head(j, _):
            @pl.when(j < KV_HALF - 1)
            def _():
                for copy in copies(j + 1):
                    copy.start()

            for copy in copies(j):
                copy.wait()
            start = pl.multiple_of(j * GROUPS * HD, GROUPS * HD)
            q = jnp.concatenate(
                [x[:, pl.ds(start + g * HD, HD)] for x in sources for g in range(GROUPS)], axis=0
            )

            def peak_of(first):
                key = keys[j, pl.ds(pl.multiple_of(first, 256), 256), :]
                scores = lax.dot_general(key, q, NT, preferred_element_type=F32) * SCALE
                inside = first + lax.broadcasted_iota(jnp.int32, scores.shape, 0) < length
                peak = jnp.max(jnp.where(inside, scores, MASKED), axis=0, keepdims=True)
                return jnp.broadcast_to(peak, (8, rows))

            m_ref[:, :rows] = peak_of(0)

            def attempt(state):
                turn = state[0]

                @pl.when(turn == 1)
                def _():
                    def more(t, carry):
                        m_ref[:, :rows] = jnp.maximum(m_ref[:, :rows], peak_of(t * 256))
                        return carry

                    lax.fori_loop(1, (length + 255) // 256, more, 0)

                def full(acc):
                    return step(j, q, 0, CHIP_SPAN, False, acc)

                def partial(acc):
                    first = jnp.int32(0)
                    for span in (2048, 1024):
                        fits = length - first >= span
                        acc = lax.cond(
                            fits,
                            functools.partial(step, j, q, first, span, False),
                            lambda a: a,
                            acc,
                        )
                        first = first + jnp.where(fits, span, 0)
                    return lax.fori_loop(
                        first // 512,
                        (length + 511) // 512,
                        lambda t, a: step(j, q, t * 512, 512, True, a),
                        acc,
                    )

                if groups == 1:
                    acc = lax.switch(
                        (length - 1) // STRIDE,
                        [
                            functools.partial(whole, j, q, span)
                            for span in range(STRIDE, CHIP_SPAN + 1, STRIDE)
                        ],
                    )
                else:
                    acc = jnp.zeros((HD + PAD, rows), F32)
                    acc = lax.cond(length == CHIP_SPAN, full, partial, acc)
                total = acc[HD : HD + 1]
                out = (acc[:HD] / total).T.astype(BF16)
                lse = jnp.broadcast_to(m_ref[0:1, :rows] + jnp.log2(total), (HD, rows)).T
                lane = lanes((count, HD)) % 32
                for i in range(groups):
                    for g in range(GROUPS):
                        part = slice((i * GROUPS + g) * count, (i * GROUPS + g + 1) * count)
                        targets[i][:, pl.ds(start + g * HD, HD)] = out[part]
                        lse_ref[i, :count] = jnp.where(
                            lane == j * GROUPS + g, lse[part], lse_ref[i, :count]
                        )
                wrong = jnp.sum(jnp.where(total < 1e30, 0.0, 1.0))
                return turn + 1, (wrong > 0.0).astype(jnp.int32)

            lax.while_loop(
                lambda state: (state[0] < 2) & (state[1] == 1),
                attempt,
                (jnp.int32(0), jnp.int32(1)),
            )
            return 0

        lax.fori_loop(0, KV_HALF, head, 0)

    for copy in copies(0):
        copy.start()
    for j in range(KV_HALF):
        turned[j, HD:, :] = jnp.ones((PAD, CHIP_SPAN), BF16)
    lse_ref[...] = jnp.zeros_like(lse_ref)
    flags = [x[:, HALF:] for x in x_refs]
    few = functools.reduce(
        jnp.logical_and, [jnp.sum(flag.astype(F32)) <= SMALL * HD for flag in flags]
    )

    @pl.when((length > 0) & few)
    def _():
        earlier = lanes((slots, slots)) < lax.broadcasted_iota(jnp.int32, (slots, slots), 0)
        places = []
        for i in range(groups):
            rank = jnp.dot(earlier.astype(BF16), flags[i], preferred_element_type=F32)
            here = (rank.astype(jnp.int32) == lanes(rank.shape)) & (flags[i].astype(F32) > 0.5)
            place = here.astype(F32).astype(BF16)[:, :SMALL]
            places.append(place)
            small_x[i] = lax.dot_general(
                place,
                x_refs[i][:, :HALF],
                (((0,), (0,)), ((), ())),
                preferred_element_type=F32,
            ).astype(BF16)
        attend(
            [small_x.at[i] for i in range(groups)], [small_o.at[i] for i in range(groups)], SMALL
        )
        for i in range(groups):
            o_refs[i][:, :HALF] = jnp.dot(
                places[i], small_o[i], preferred_element_type=F32
            ).astype(BF16)
            lse = split_three(lse_ref[i, :SMALL], lanes((SMALL, HD)))
            o_refs[i][:, HALF:] = jnp.dot(places[i], lse, preferred_element_type=F32).astype(BF16)

    @pl.when((length > 0) & jnp.logical_not(few))
    def _():
        attend(x_refs, o_refs, slots)
        for i in range(groups):
            o_refs[i][:, HALF:] = split_three(lse_ref[i], lanes((slots, HD)))

    @pl.when(length == 0)
    def _():
        for copy in copies(0):
            copy.wait()
        for o_ref in o_refs:
            o_ref[:, :HALF] = jnp.zeros((slots, HALF), BF16)
            o_ref[:, HALF:] = split_three(
                jnp.full((slots, HD), MASKED, F32), lanes((slots, HD))
            )


def prefix_partial(xs, meta, k_own, k_peer, v_own, v_peer):
    groups = len(xs)
    count = xs[0].shape[0]
    inside = pl.BlockSpec(memory_space=pltpu.VMEM)
    return pl.pallas_call(
        functools.partial(prefix_kernel, groups=groups),
        in_specs=[pl.BlockSpec(memory_space=pltpu.SMEM)]
        + [inside] * groups
        + [pl.BlockSpec(memory_space=pl.ANY)] * 4,
        out_specs=[inside] * groups,
        out_shape=[jax.ShapeDtypeStruct((count, WIDE), BF16)] * groups,
        scratch_shapes=[
            pltpu.VMEM((KV_HALF, CHIP_SPAN, HD), BF16),
            pltpu.VMEM((KV_HALF, HD + PAD, CHIP_SPAN), BF16),
            pltpu.VMEM((8, groups * GROUPS * count), F32),
            pltpu.VMEM((groups, count, HD), F32),
            pltpu.VMEM((groups, SMALL, HALF), BF16),
            pltpu.VMEM((groups, SMALL, HALF), BF16),
            pltpu.SemaphoreType.DMA((KV_HALF, 4)),
        ],
        compiler_params=pltpu.CompilerParams(vmem_limit_bytes=56 << 20),
        cost_estimate=pl.CostEstimate(
            flops=16 * groups * count * HEADS_HALF * CHIP_SPAN * HD,
            bytes_accessed=16 * BLOCK * KV_HALF * HD,
            transcendentals=groups * count * HEADS_HALF * CHIP_SPAN,
        ),
        name="prefix_partial",
    )(meta, *xs, k_own, k_peer, v_own, v_peer)


def merge_kernel(*refs):
    parts, out_ref = refs[:-1], refs[-1]
    sums = [join_three(part[:, HALF:]) for part in parts]
    top = functools.reduce(jnp.maximum, sums)
    shares = [jnp.exp2(s - top) for s in sums]
    whole = functools.reduce(jnp.add, shares)
    shares = [s / whole for s in shares]
    for h in range(HEADS_HALF):
        block = slice(h * HD, (h + 1) * HD)
        out = None
        for part, share in zip(parts, shares):
            term = part[:, block].astype(F32) * share[:, h : h + 1]
            out = term if out is None else out + term
        out_ref[:, block] = out.astype(BF16)
    lane = lanes(top.shape)
    lse = jnp.where(lane < 32, top + jnp.log2(whole), 0.0)
    lse = lse + pltpu.roll(lse, 32, 1) + pltpu.roll(lse, 64, 1)
    out_ref[:, HALF:] = split_three(lse, lane)


def merge(*parts):
    return pl.pallas_call(
        merge_kernel,
        out_shape=jax.ShapeDtypeStruct(parts[0].shape, BF16),
        name="merge",
    )(*parts)


def finish_kernel(back_ref, pick_ref, o_ref, lse_ref, out_ref):
    slots = back_ref.shape[0]
    rows = o_ref.shape[0]
    picked = jnp.dot(pick_ref[:, :slots], back_ref[...], preferred_element_type=F32)
    for half in range(2):
        part = picked[half * rows : (half + 1) * rows]
        prefix_lse = join_three(part[:, HALF:])
        suffix_lse = lse_ref[...]
        if half:
            suffix_lse = pltpu.roll(suffix_lse, 96, 1)
        top = jnp.maximum(prefix_lse, suffix_lse)
        prefix_share = jnp.exp2(prefix_lse - top)
        suffix_share = jnp.exp2(suffix_lse - top)
        whole = prefix_share + suffix_share
        prefix_share = prefix_share / whole
        suffix_share = suffix_share / whole
        for h in range(HEADS_HALF):
            block = slice(h * HD, (h + 1) * HD)
            place = slice(half * HALF + h * HD, half * HALF + (h + 1) * HD)
            out_ref[:, place] = (
                part[:, block] * prefix_share[:, h : h + 1]
                + o_ref[:, place] * suffix_share[:, h : h + 1]
            ).astype(BF16)


def finish(back, pick, suffix_out, suffix_lse):
    return pl.pallas_call(
        finish_kernel,
        out_shape=jax.ShapeDtypeStruct(suffix_out.shape, BF16),
        name="finish",
    )(back, pick, suffix_out, suffix_lse)


def ring(shift):
    return [(i, (i + shift) % 4) for i in range(4)]


SWAP = [(0, 1), (1, 0)]


def local(
    queries,
    prefix_ids,
    prefix_lengths,
    prefix_keys,
    prefix_values,
    suffix_keys,
    suffix_values,
    suffix_lengths,
):
    core = lax.axis_index("c")
    chip = lax.axis_index("y")
    keys = prefix_keys[0]
    values = prefix_values[0]
    slots = 2 * CAP * OWNERS
    leaving, pick = dispatch(queries, prefix_ids)
    v_own, v_other, k_other = prepare(core.reshape(1).astype(jnp.int32), keys, values)
    arrived = lax.all_to_all(
        leaving.reshape(2 * OWNERS, CAP, WIDE), PLANE, split_axis=0, concat_axis=0, tiled=True
    ).reshape(slots, WIDE)
    arrived, late, v_other, k_other = lax.optimization_barrier(
        (arrived, queries, v_other, k_other)
    )
    v_peer = lax.ppermute(v_other, "c", SWAP)
    k_peer = lax.ppermute(k_other, "c", SWAP)
    from_left = lax.ppermute(arrived, "y", ring(1))
    from_right = lax.ppermute(arrived, "y", ring(3))
    suffix_out, suffix_lse = suffix(late, suffix_keys, suffix_values, suffix_lengths)
    from_left, from_right, suffix_out, suffix_lse, far = lax.optimization_barrier(
        (from_left, from_right, suffix_out, suffix_lse, arrived)
    )
    from_far = lax.ppermute(far, "y", ring(2))

    count = jnp.clip(prefix_lengths[0] - chip * CHIP_SPAN, 0, CHIP_SPAN)
    meta = jnp.stack([count, core]).astype(jnp.int32)
    work = functools.partial(
        prefix_partial, meta=meta, k_own=keys, k_peer=k_peer, v_own=v_own, v_peer=v_peer
    )
    for_left, for_right = work([from_left, from_right])
    back_left = lax.ppermute(for_left, "y", ring(3))
    back_right = lax.ppermute(for_right, "y", ring(1))
    (for_far,) = work([from_far])
    back_far = lax.ppermute(for_far, "y", ring(2))
    (for_self,) = work([arrived])
    merged = merge(for_self, back_left, back_right, back_far)
    back = lax.all_to_all(
        merged.reshape(2 * OWNERS, CAP, WIDE), PLANE, split_axis=0, concat_axis=0, tiled=True
    ).reshape(slots, WIDE)
    return finish(back, pick, suffix_out, suffix_lse)


def solution(mesh):
    fine = Mesh(mesh.devices.reshape(4, 4, 4, 2), AXES)
    rows = P(AXES)
    placed = (
        P(AXES, None),
        rows,
        P(("z", "x")),
        P(("z", "x"), None, ("y", "c"), None),
        P(("z", "x"), None, ("y", "c"), None),
        P(AXES, None, None, None),
        P(AXES, None, None, None),
        rows,
    )
    return jax.shard_map(
        local, mesh=fine, in_specs=placed, out_specs=P(AXES, None), check_vma=False
    )
```
